32 devices in a mesh: row: 4 (over y, core), col: 8 (over z, x).
Axes of the slice: x: 2, y: 2, z: 4, core: 2. Of those that a mesh axis runs over, the one named last changes fastest.
Arguments:
- act_sketch: bfloat16 [2, 2048, 256], P(None, 'row'), may hold values from -6 to 6
- grad_sketch: bfloat16 [2, 2048, 256], P(None, 'row'), may hold values from -6 to 6
- targets: float32 [2048, 256], P('row'), may hold values from -6 to 6
Outputs:
- residual: float32 [2048, 256], P(('row', 'col'))
The draws below stay inside these ranges and needn't reach their ends.
All inputs are finite; a program needn't handle non-finite values.
Results may differ from the reference program's by a relative error of at most 0.014.
The reference program's roundings to bfloat16 on the way (of `kernel`) count: a program that leaves them out, or rounds other values in their place, can miss the bound.
Values may be sent and summed in bfloat16 or wider, within the bound.
No kernel may reach another device: no remote copies, remote signals or barrier semaphores. Data moves between devices by JAX's collectives and lax.ppermute only.
A program may use at most 64 MiB of HBM per device.

```python
import math
import jax
import jax.numpy as jnp
from jax import lax

W = 256
OUT = 256
LAYERS = 2
ITERS = 8
N = 2048
CB = 256


def block_levels(stream_key, extent, shards, smallest, largest):
    loudness = 1.0
    for axis_at, shards_of in shards:
        heights = jax.random.uniform(jax.random.fold_in(jax.random.fold_in(stream_key, 6), axis_at), (shards_of,), jnp.float32, smallest / len(shards), largest / len(shards))
        loudness = loudness * jnp.repeat(jnp.exp(heights), extent[axis_at] // shards_of).reshape((-1,) + (1,) * (len(extent) - 1 - axis_at))
    return loudness


def scatter_about(stream_key, shape, deviation, bound, shards=(), kind=jnp.bfloat16):
    gain = block_levels(stream_key, shape, shards, -0.22, 0.18) if shards else 1.0
    values = jax.random.normal(stream_key, shape, jnp.float32) * deviation * gain
    return jnp.minimum(jnp.maximum(values, -bound), bound).astype(kind)


def setup_inputs(seed: int = 0) -> dict:
    arg_keys = jax.random.split(jax.random.key(seed), 4)
    act_sketch = scatter_about(arg_keys[0], (LAYERS, N, W), 1.0, 6.0, ((1, 4),))
    grad_sketch = scatter_about(arg_keys[1], (LAYERS, N, W), 1.0, 6.0, ((1, 4),))
    targets = scatter_about(arg_keys[2], (N, OUT), 1.0, 6.0, ((0, 4),), jnp.float32)
    return {"act_sketch": act_sketch, "grad_sketch": grad_sketch, "targets": targets}


def reference(act_sketch, grad_sketch, targets):
    scale = W * math.sqrt(N) / 4.0
    blocks = N // CB
    act_all = act_sketch.astype(jnp.float32)
    grad_all = grad_sketch.astype(jnp.float32)

    def kernel_block(index):
        start = (index * CB).astype(jnp.int32)
        total = jnp.zeros((CB, N), jnp.float32)
        for layer in range(LAYERS):
            act_rows = lax.dynamic_slice_in_dim(act_all[layer], start, CB, 0)
            grad_rows = lax.dynamic_slice_in_dim(grad_all[layer], start, CB, 0)
            act_gram = jnp.dot(act_rows, act_all[layer].T)
            grad_gram = jnp.dot(grad_rows, grad_all[layer].T)
            total = total + act_gram * grad_gram
        return (total / scale).astype(jnp.bfloat16)
    kernel = lax.map(kernel_block, jnp.arange(blocks, dtype=jnp.int32))
    residual = targets
    for step in range(ITERS):
        squashed = jnp.tanh(residual).astype(jnp.bfloat16).astype(jnp.float32)

        def apply_block(kblock):
            return jnp.dot(kblock.astype(jnp.float32), squashed)
        update = lax.map(apply_block, kernel).reshape(N, OUT)
        residual = residual - 0.05 * update
    return residual
```

```python
import functools
import math

import jax
import jax.numpy as jnp
from jax import lax
from jax.experimental import pallas as pl
from jax.experimental.pallas import tpu as pltpu
from jax.sharding import PartitionSpec as P

ITERS = 8
RATE = 0.05
TILE = 256
VMEM_LIMIT = 56 * 2**20
NT = (((1,), (1,)), ((), ()))


def broadcast(value, axis, source):
    kept = jnp.where(lax.axis_index(axis) == source, value, 0).astype(value.dtype)
    return lax.psum(kept, axis)


def gram_pair(left, right):
    return lax.dot_general(left, right, NT, preferred_element_type=jnp.float32)


def split_body(act_sketch, grad_sketch, targets):
    row_count = lax.axis_size("row")
    col_count = lax.axis_size("col")
    ratio = col_count // row_count
    examples = targets.shape[0]
    col_block = examples // ratio
    share_rows = examples // col_count
    col_place = lax.axis_index("col")
    root = col_place // ratio
    offset = col_place % ratio * col_block
    scale = act_sketch.shape[2] * math.sqrt(examples * row_count) / 4.0

    def pick(array, dim):
        return lax.dynamic_slice_in_dim(array, offset, col_block, dim)

    act_cols, grad_cols = (
        broadcast(pick(act_sketch, 1), "row", root),
        broadcast(pick(grad_sketch, 1), "row", root),
    )
    total = jnp.zeros((examples, col_block), jnp.float32)
    for layer in range(act_sketch.shape[0]):
        act_gram = gram_pair(act_sketch[layer], act_cols[layer])
        grad_gram = gram_pair(grad_sketch[layer], grad_cols[layer])
        total = total + act_gram * grad_gram
    kernel = (total / scale).astype(jnp.bfloat16)
    state = targets
    for step in range(ITERS):
        panel = broadcast(
            jnp.tanh(pick(state, 0)).astype(jnp.bfloat16), "row", root
        )
        partial_value = jnp.dot(kernel, panel, preferred_element_type=jnp.float32)
        summed = lax.psum(partial_value, "col")
        state = state - RATE * summed
    return lax.dynamic_slice_in_dim(state, col_place * share_rows, share_rows, 0)


def pack_kernel(act, grad, targets, packed):
    layers, _, width = act.shape
    for layer in range(layers):
        packed[:, layer * width : (layer + 1) * width] = act[layer]
        packed[:, (layers + layer) * width : (layers + layer + 1) * width] = grad[layer]
    value = targets[...]
    high = value.astype(jnp.bfloat16)
    out = value.shape[1]
    at = 2 * layers * width
    packed[:, at : at + out] = high
    packed[:, at + out : at + 2 * out] = (value - high.astype(jnp.float32)).astype(
        jnp.bfloat16
    )


def pack(act, grad, targets):
    layers, rows, width = act.shape
    out = targets.shape[1]
    return pl.pallas_call(
        pack_kernel,
        out_shape=jax.ShapeDtypeStruct(
            (rows, 2 * layers * width + 2 * out), jnp.bfloat16
        ),
        in_specs=[pl.BlockSpec(memory_space=pltpu.VMEM)] * 3,
        out_specs=pl.BlockSpec(memory_space=pltpu.VMEM),
        compiler_params=pltpu.CompilerParams(vmem_limit_bytes=VMEM_LIMIT),
    )(act, grad, targets)


def descent_kernel(layers, width, out, share, scale, pieces, *refs):
    place = refs[0]
    sources = refs[1 : 1 + pieces]
    result = refs[1 + pieces]
    data, kernel, residual, squashed, sems = refs[2 + pieces :]
    examples = data.shape[0]
    tiles = examples // TILE
    copies, ends, at = [], [], 0
    for index, source in enumerate(sources):
        rows = source.shape[0]
        copy = pltpu.make_async_copy(
            source, data.at[pl.ds(at, rows), :], sems.at[index]
        )
        copy.start()
        copies.append(copy)
        at += rows
        ends.append(at)

    waited = 0
    target_at = 2 * layers * width
    for j in range(tiles):
        cols = slice(j * TILE, (j + 1) * TILE)
        while waited < pieces and (waited == 0 or ends[waited - 1] < (j + 1) * TILE):
            copies[waited].wait()
            waited += 1
        value = data[cols, target_at : target_at + out].astype(jnp.float32) + data[
            cols, target_at + out : target_at + 2 * out
        ].astype(jnp.float32)
        residual[cols, :] = value
        squashed[0, cols, :] = jnp.tanh(value).astype(jnp.bfloat16)
        for i in range(j + 1):
            rows = slice(i * TILE, (i + 1) * TILE)
            total = None
            for layer in range(layers):
                a = slice(layer * width, (layer + 1) * width)
                g = slice((layers + layer) * width, (layers + layer + 1) * width)
                term = gram_pair(data[rows, a], data[cols, a]) * gram_pair(
                    data[rows, g], data[cols, g]
                )
                total = term if total is None else total + term
            block = (total * (1.0 / scale)).astype(jnp.bfloat16)
            kernel[rows, cols] = block
            if i != j:
                kernel[cols, rows] = block.T

    for step in range(ITERS - 1):
        now, later = step % 2, (step + 1) % 2
        for i in range(tiles):
            rows = slice(i * TILE, (i + 1) * TILE)
            update = jnp.dot(
                kernel[rows, :], squashed[now], preferred_element_type=jnp.float32
            )
            value = residual[rows, :] - RATE * update
            residual[rows, :] = value
            squashed[later, rows, :] = jnp.tanh(value).astype(jnp.bfloat16)
    mine = pl.ds(pl.multiple_of(place[0] * share, share), share)
    update = jnp.dot(
        kernel[mine, :],
        squashed[(ITERS - 1) % 2],
        preferred_element_type=jnp.float32,
    )
    result[...] = residual[mine, :] - RATE * update


def descend(place, sources, layers, width, out, share):
    examples = sum(source.shape[0] for source in sources)
    scale = width * math.sqrt(examples) / 4.0
    pieces = len(sources)
    return pl.pallas_call(
        functools.partial(descent_kernel, layers, width, out, share, scale, pieces),
        out_shape=jax.ShapeDtypeStruct((share, out), jnp.float32),
        in_specs=[pl.BlockSpec(memory_space=pltpu.SMEM)]
        + [pl.BlockSpec(memory_space=pl.ANY)] * pieces,
        out_specs=pl.BlockSpec(memory_space=pltpu.VMEM),
        scratch_shapes=[
            pltpu.VMEM((examples, sources[0].shape[1]), jnp.bfloat16),
            pltpu.VMEM((examples, examples), jnp.bfloat16),
            pltpu.VMEM((examples, out), jnp.float32),
            pltpu.VMEM((2, examples, out), jnp.bfloat16),
            pltpu.SemaphoreType.DMA((pieces,)),
        ],
        compiler_params=pltpu.CompilerParams(vmem_limit_bytes=VMEM_LIMIT),
    )(place, *sources)


def whole_body(act_sketch, grad_sketch, targets):
    row_count = lax.axis_size("row")
    col_count = lax.axis_size("col")
    layers, rows, width = act_sketch.shape
    out = targets.shape[1]
    packed = pack(act_sketch, grad_sketch, targets)

    def twin(value):
        return lax.ppermute(value, "row", [(i, i ^ 1) for i in range(row_count)])

    pieces = [packed, twin(packed)]
    for hop in range(2, row_count, 2):
        other = lax.ppermute(
            packed, "row", [(i, (i + hop) % row_count) for i in range(row_count)]
        )
        pieces += [other, twin(other)]
    place = lax.axis_index("col").astype(jnp.int32).reshape(1)
    return descend(place, pieces, layers, width, out, rows // col_count)


def fits(mesh, act_sketch, targets):
    layers, examples, width = act_sketch.shape
    out = targets.shape[1]
    share = examples // (mesh.shape["row"] * mesh.shape["col"])
    held = examples * (2 * examples + 4 * layers * width + 12 * out)
    return (
        held <= VMEM_LIMIT * 3 // 4
        and mesh.shape["row"] % 2 == 0
        and examples // mesh.shape["row"] % TILE == 0
        and share % 16 == 0
    )


def solution(mesh):
    def step(act_sketch, grad_sketch, targets):
        body = whole_body if fits(mesh, act_sketch, targets) else split_body
        return jax.shard_map(
            body,
            mesh=mesh,
            in_specs=(P(None, "row", None), P(None, "row", None), P("row", None)),
            out_specs=P(("row", "col"), None),
            check_vma=False,
        )(act_sketch, grad_sketch, targets)

    return step
```

```python
import functools
import math

import jax
import jax.numpy as jnp
from jax import lax
from jax.experimental import pallas as pl
from jax.experimental.pallas import tpu as pltpu
from jax.sharding import PartitionSpec as P

ITERS = 8
RATE = 0.05
TILE = 256
STATE_LIMIT = 32 * 2**20
SCOPED_LIMIT = 16 * 2**20
NT = (((1,), (1,)), ((), ()))


def broadcast(value, axis, source):
    kept = jnp.where(lax.axis_index(axis) == source, value, 0).astype(value.dtype)
    return lax.psum(kept, axis)


def gram_pair(left, right):
    return lax.dot_general(left, right, NT, preferred_element_type=jnp.float32)


def split_body(act_sketch, grad_sketch, targets):
    row_count = lax.axis_size("row")
    col_count = lax.axis_size("col")
    ratio = col_count // row_count
    examples = targets.shape[0]
    col_block = examples // ratio
    share_rows = examples // col_count
    col_place = lax.axis_index("col")
    root = col_place // ratio
    offset = col_place % ratio * col_block
    scale = act_sketch.shape[2] * math.sqrt(examples * row_count) / 4.0

    def pick(array, dim):
        return lax.dynamic_slice_in_dim(array, offset, col_block, dim)

    act_cols, grad_cols = (
        broadcast(pick(act_sketch, 1), "row", root),
        broadcast(pick(grad_sketch, 1), "row", root),
    )
    total = jnp.zeros((examples, col_block), jnp.float32)
    for layer in range(act_sketch.shape[0]):
        act_gram = gram_pair(act_sketch[layer], act_cols[layer])
        grad_gram = gram_pair(grad_sketch[layer], grad_cols[layer])
        total = total + act_gram * grad_gram
    kernel = (total / scale).astype(jnp.bfloat16)
    state = targets
    for step in range(ITERS):
        panel = broadcast(
            jnp.tanh(pick(state, 0)).astype(jnp.bfloat16), "row", root
        )
        partial_value = jnp.dot(kernel, panel, preferred_element_type=jnp.float32)
        summed = lax.psum(partial_value, "col")
        state = state - RATE * summed
    return lax.dynamic_slice_in_dim(state, col_place * share_rows, share_rows, 0)


def kind_of(place):
    upper = (place // 2) % 2
    return (place % 2 + upper) % 2 * 2 + upper


def pack_kernel(takes, act, grad, targets, *refs):
    count = len(takes)
    packed, (token, wide, sem, wide_sem) = refs[:count], refs[count:]
    token[...] = jnp.zeros_like(token)
    layers, rows, width = act.shape
    out = targets.shape[1]
    quarter = rows // 4
    kind = kind_of(lax.axis_index("col"))
    copies, late, at = [], [], 0
    for ref, (flip, skip) in zip(packed, takes):
        size = ref.shape[0]
        quarter_at = (kind + flip - 2 * flip * (kind % 2)) * quarter + skip
        source = pl.ds(pl.multiple_of(quarter_at, 16), size)
        copy = pltpu.make_async_copy(
            targets.at[source, :], wide.at[pl.ds(at, size), :], wide_sem
        )
        copy.start()
        late.append(copy)
        at += size
        for layer in range(layers):
            for side, array in enumerate((act, grad)):
                lane = (side * layers + layer) * width
                copy = pltpu.make_async_copy(
                    array.at[layer, source, :], ref.at[:, pl.ds(lane, width)], sem
                )
                copy.start()
                copies.append(copy)
    for copy in late:
        copy.wait()
    at, lane = 0, 2 * layers * width
    for ref in packed:
        size = ref.shape[0]
        value = wide[at : at + size, :]
        high = value.astype(jnp.bfloat16)
        ref[:, lane : lane + out] = high
        ref[:, lane + out : lane + 2 * out] = (
            value - high.astype(jnp.float32)
        ).astype(jnp.bfloat16)
        at += size
    for copy in copies:
        copy.wait()


def pack(act, grad, targets, sizes, takes):
    layers, rows, width = act.shape
    out = targets.shape[1]
    lanes = 2 * layers * width + 2 * out
    return pl.pallas_call(
        functools.partial(pack_kernel, takes),
        out_shape=[jax.ShapeDtypeStruct((s, lanes), jnp.bfloat16) for s in sizes]
        + [TOKEN],
        in_specs=[pl.BlockSpec(memory_space=pltpu.HBM)] * 3,
        out_specs=[pl.BlockSpec(memory_space=pltpu.VMEM)] * (len(sizes) + 1),
        scratch_shapes=[
            pltpu.VMEM((sum(sizes), out), jnp.float32),
            pltpu.SemaphoreType.DMA(()),
            pltpu.SemaphoreType.DMA(()),
        ],
        compiler_params=pltpu.CompilerParams(vmem_limit_bytes=SCOPED_LIMIT),
    )(act, grad, targets)


def build(layers, scale, low, high, data, kernel):
    width = data.shape[1] // (2 * layers)
    for at in range(low, high, TILE):
        cols = slice(at, at + TILE)
        for row_at in range(0, at + TILE, TILE):
            rows = slice(row_at, row_at + TILE)
            total = None
            for layer in range(layers):
                a = slice(layer * width, (layer + 1) * width)
                g = slice((layers + layer) * width, (layers + layer + 1) * width)
                term = gram_pair(data[rows, a], data[cols, a]) * gram_pair(
                    data[rows, g], data[cols, g]
                )
                total = term if total is None else total + term
            block = (total * (1.0 / scale)).astype(jnp.bfloat16)
            kernel[rows, cols] = block
            if row_at != at:
                kernel[cols, rows] = block.T


def begin(low, high, kernel, residual, squashed):
    for at in range(low, high, TILE):
        cols = slice(at, at + TILE)
        squashed[cols, :] = jnp.tanh(residual[cols, :]).astype(jnp.bfloat16)
    for at in range(0, high, TILE):
        rows = slice(at, at + TILE)
        cols = slice(low if at < low else 0, high)
        residual[rows, :] -= RATE * jnp.dot(
            kernel[rows, cols], squashed[cols, :], preferred_element_type=jnp.float32
        )


def unpack_block(act, grad, low, data):
    layers, rows, width = act.shape
    for layer in range(layers):
        for side, array in enumerate((act, grad)):
            lane = (side * layers + layer) * width
            data[low : low + rows, lane : lane + width] = array[layer]


def unpack_pieces(pieces, low, data, residual):
    sketch, out = data.shape[1], residual.shape[1]
    for piece in pieces:
        high = low + piece.shape[0]
        data[low:high, :] = piece[:, :sketch]
        residual[low:high, :] = piece[:, sketch : sketch + out].astype(
            jnp.float32
        ) + piece[:, sketch + out :].astype(jnp.float32)
        low = high
    return low


def first_kernel(layers, scale, *refs):
    block, beside, state = refs[:3], refs[3:6], refs[7:11]
    token, sem = refs[11:]
    data, kernel, residual, squashed = state
    act, grad, targets = block
    rows, width = act.shape[1:]
    copies = [pltpu.make_async_copy(targets, residual.at[pl.ds(0, rows), :], sem)]
    for layer in range(layers):
        for side, array in enumerate((act, grad)):
            lane = (side * layers + layer) * width
            copies.append(
                pltpu.make_async_copy(
                    array.at[layer], data.at[pl.ds(0, rows), pl.ds(lane, width)], sem
                )
            )
    for copy in copies:
        copy.start()
    unpack_block(*beside[:2], rows, data)
    residual[rows : 2 * rows, :] = beside[2][...]
    for copy in copies:
        copy.wait()
    build(layers, scale, 0, 2 * rows, data, kernel)
    begin(0, 2 * rows, kernel, residual, squashed)
    token[...] = jnp.zeros_like(token)


def stage_kernel(layers, scale, low, count, *refs):
    pieces, state, token = refs[:count], refs[-5:-1], refs[-1]
    data, kernel, residual, squashed = state
    high = unpack_pieces(pieces, low, data, residual)
    build(layers, scale, low, high, data, kernel)
    begin(low, high, kernel, residual, squashed)
    token[...] = jnp.zeros_like(token)


def last_kernel(layers, scale, low, count, *refs):
    pieces, state = refs[:count], refs[count : count + 4]
    result, other = refs[count + 4 :]
    data, kernel, residual, squashed = state
    share = result.shape[0]
    high = unpack_pieces(pieces, low, data, residual)
    build(layers, scale, low, high, data, kernel)
    begin(low, high, kernel, residual, squashed)
    panels = (squashed, other)
    for at in range(0, high, TILE):
        rows = slice(at, at + TILE)
        other[rows, :] = jnp.tanh(residual[rows, :]).astype(jnp.bfloat16)
    for step in range(1, ITERS - 1):
        now, later = panels[step % 2], panels[(step + 1) % 2]
        for at in range(0, high, TILE):
            rows = slice(at, at + TILE)
            update = jnp.dot(
                kernel[rows, :], now[...], preferred_element_type=jnp.float32
            )
            value = residual[rows, :] - RATE * update
            residual[rows, :] = value
            later[rows, :] = jnp.tanh(value).astype(jnp.bfloat16)
    place = lax.axis_index("col")
    mine = pl.ds(pl.multiple_of(place * share, share), share)
    update = jnp.dot(
        kernel[mine, :],
        panels[(ITERS - 1) % 2][...],
        preferred_element_type=jnp.float32,
    )
    result[...] = residual[mine, :] - RATE * update


def hold_kernel(*refs):
    pass


IN_VMEM = pl.BlockSpec(memory_space=pltpu.VMEM)
IN_HBM = pl.BlockSpec(memory_space=pltpu.HBM)
PARAMS = pltpu.CompilerParams(vmem_limit_bytes=SCOPED_LIMIT)
SMALL = pltpu.CompilerParams(vmem_limit_bytes=SCOPED_LIMIT // 4)
TOKEN = jax.ShapeDtypeStruct((8, 128), jnp.float32)


def cost(layers, width, out, low, high):
    grown = high * high - low * low
    return pl.CostEstimate(
        flops=grown * (2 * layers * width + 2 * out),
        bytes_accessed=grown,
        transcendentals=(high - low) * out,
    )


def state_shapes(examples, sketch, out):
    return [
        pltpu.VMEM((examples, sketch), jnp.bfloat16),
        pltpu.VMEM((examples, examples), jnp.bfloat16),
        pltpu.VMEM((examples, out), jnp.float32),
        pltpu.VMEM((examples, out), jnp.bfloat16),
    ]


def after(value, *tokens):
    return pl.pallas_call(
        hold_kernel,
        out_shape=jax.ShapeDtypeStruct(value.shape, value.dtype),
        in_specs=[IN_HBM] * (1 + len(tokens)),
        out_specs=IN_HBM,
        input_output_aliases={0: 0},
        compiler_params=SMALL,
    )(value, *tokens)


def join_kernel(one, other, *refs):
    joined = refs[-1]
    rows = one.shape[0]
    joined[:rows, :] = one[...]
    joined[rows:, :] = other[...]


def join(one, other, *tokens):
    return pl.pallas_call(
        join_kernel,
        out_shape=jax.ShapeDtypeStruct((2 * one.shape[0], one.shape[1]), one.dtype),
        in_specs=[IN_VMEM] * 2 + [IN_HBM] * len(tokens),
        out_specs=IN_VMEM,
        compiler_params=SMALL,
    )(one, other, *tokens)


def whole_body(act_sketch, grad_sketch, targets):
    row_count = lax.axis_size("row")
    col_count = lax.axis_size("col")
    layers, rows, width = act_sketch.shape
    out = targets.shape[1]
    examples = rows * row_count
    share = rows // col_count
    scale = width * math.sqrt(examples) / 4.0
    quarter, eighth = rows // 4, rows // 8

    def twin(value):
        return lax.ppermute(value, "row", [(i, i ^ 1) for i in range(row_count)])

    def across(value):
        return lax.ppermute(value, "row", [(i, i ^ 2) for i in range(row_count)])

    def near(value):
        return lax.ppermute(value, "col", [(i, i ^ 1) for i in range(col_count)])

    def far(value):
        return lax.ppermute(value, "col", [(i, i ^ 2) for i in range(col_count)])

    shapes = state_shapes(examples, 2 * layers * width, out)

    def stage(state, low, pieces):
        count = len(pieces)
        *state, token = pl.pallas_call(
            functools.partial(stage_kernel, layers, scale, low, count),
            out_shape=[*shapes, TOKEN],
            in_specs=[IN_VMEM] * (count + 4),
            out_specs=[IN_VMEM] * 5,
            input_output_aliases={count + i: i for i in range(4)},
            compiler_params=PARAMS,
            cost_estimate=cost(layers, width, out, low, low + 2 * quarter),
        )(*pieces, *state)
        return state, token

    own = [
        pltpu.with_memory_space_constraint(array, pltpu.HBM)
        for array in (act_sketch, grad_sketch, targets)
    ]
    first, second, third, token = pack(
        *own,
        (eighth, eighth, quarter),
        ((0, 0), (0, eighth), (1, 0)),
    )
    first, second = across(first), across(second)
    beside = twin(act_sketch), twin(grad_sketch), twin(targets)
    third = across(after(third, *beside))
    *state, token = pl.pallas_call(
        functools.partial(first_kernel, layers, scale),
        out_shape=[*shapes, TOKEN],
        in_specs=[IN_HBM] * 3 + [IN_VMEM] * 3 + [IN_HBM],
        out_specs=[IN_VMEM] * 5,
        scratch_shapes=[pltpu.SemaphoreType.DMA(())],
        compiler_params=PARAMS,
        cost_estimate=cost(layers, width, out, 0, 2 * rows),
    )(*own, *beside, token)

    first, second = after(first, token), after(second, token)
    near_first, far_first = near(first), far(first)
    near_second, far_second = near(second), far(second)
    low = 2 * rows
    pieces = join(first, second, far_first)
    state, token = stage(state, low, [pieces, twin(pieces)])
    low += 2 * quarter
    pieces = join(near_first, far_first)
    state, token = stage(state, low, [pieces, twin(pieces)])
    low += 2 * quarter
    pieces = join(near_second, far_second, token)
    state, token = stage(state, low, [third, twin(third)])
    low += 2 * quarter
    pieces = [pieces, twin(pieces)]
    count = len(pieces)
    return pl.pallas_call(
        functools.partial(last_kernel, layers, scale, low, count),
        out_shape=jax.ShapeDtypeStruct((share, out), jnp.float32),
        in_specs=[IN_VMEM] * (count + 4),
        out_specs=IN_VMEM,
        scratch_shapes=[pltpu.VMEM((examples, out), jnp.bfloat16)],
        compiler_params=PARAMS,
    )(*pieces, *state)


def fits(mesh, act_sketch, targets):
    layers, examples, width = act_sketch.shape
    row_count, col_count = mesh.shape["row"], mesh.shape["col"]
    state = examples * (2 * examples + 4 * layers * width + 6 * targets.shape[1])
    return (
        state <= STATE_LIMIT
        and row_count == 4
        and col_count % 4 == 0
        and examples % (row_count * 2 * TILE) == 0
        and examples % (row_count * col_count * 16) == 0
    )


def solution(mesh):
    def step(act_sketch, grad_sketch, targets):
        body = whole_body if fits(mesh, act_sketch, targets) else split_body
        return jax.shard_map(
            body,
            mesh=mesh,
            in_specs=(P(None, "row", None), P(None, "row", None), P("row", None)),
            out_specs=P(("row", "col"), None),
            check_vma=False,
        )(act_sketch, grad_sketch, targets)

    return step
```

```python
import functools
import math

import jax
import jax.numpy as jnp
from jax import lax
from jax.experimental import pallas as pl
from jax.experimental.pallas import tpu as pltpu
from jax.sharding import PartitionSpec as P

ITERS = 8
RATE = 0.05
TILE = 256
STATE_LIMIT = 32 * 2**20
SCOPED_LIMIT = 16 * 2**20
NT = (((1,), (1,)), ((), ()))


def broadcast(value, axis, source):
    kept = jnp.where(lax.axis_index(axis) == source, value, 0).astype(value.dtype)
    return lax.psum(kept, axis)


def gram_pair(left, right):
    return lax.dot_general(left, right, NT, preferred_element_type=jnp.float32)


def split_body(act_sketch, grad_sketch, targets):
    row_count = lax.axis_size("row")
    col_count = lax.axis_size("col")
    ratio = col_count // row_count
    examples = targets.shape[0]
    col_block = examples // ratio
    share_rows = examples // col_count
    col_place = lax.axis_index("col")
    root = col_place // ratio
    offset = col_place % ratio * col_block
    scale = act_sketch.shape[2] * math.sqrt(examples * row_count) / 4.0

    def pick(array, dim):
        return lax.dynamic_slice_in_dim(array, offset, col_block, dim)

    act_cols, grad_cols = (
        broadcast(pick(act_sketch, 1), "row", root),
        broadcast(pick(grad_sketch, 1), "row", root),
    )
    total = jnp.zeros((examples, col_block), jnp.float32)
    for layer in range(act_sketch.shape[0]):
        act_gram = gram_pair(act_sketch[layer], act_cols[layer])
        grad_gram = gram_pair(grad_sketch[layer], grad_cols[layer])
        total = total + act_gram * grad_gram
    kernel = (total / scale).astype(jnp.bfloat16)
    state = targets
    for step in range(ITERS):
        panel = broadcast(
            jnp.tanh(pick(state, 0)).astype(jnp.bfloat16), "row", root
        )
        partial_value = jnp.dot(kernel, panel, preferred_element_type=jnp.float32)
        summed = lax.psum(partial_value, "col")
        state = state - RATE * summed
    return lax.dynamic_slice_in_dim(state, col_place * share_rows, share_rows, 0)


def kind_of(place):
    upper = (place // 2) % 2
    return (place % 2 + upper) % 2 * 2 + upper


def pack_kernel(takes, act, grad, targets, *refs):
    count = len(takes)
    packed, (token, wide, sem, wide_sem) = refs[:count], refs[count:]
    token[...] = jnp.zeros_like(token)
    layers, rows, width = act.shape
    out = targets.shape[1]
    quarter = rows // 4
    kind = kind_of(lax.axis_index("col"))
    copies, late, at = [], [], 0
    for ref, (flip, skip) in zip(packed, takes):
        size = ref.shape[0]
        quarter_at = (kind + flip - 2 * flip * (kind % 2)) * quarter + skip
        source = pl.ds(pl.multiple_of(quarter_at, 16), size)
        copy = pltpu.make_async_copy(
            targets.at[source, :], wide.at[pl.ds(at, size), :], wide_sem
        )
        copy.start()
        late.append(copy)
        at += size
        for layer in range(layers):
            for side, array in enumerate((act, grad)):
                lane = (side * layers + layer) * width
                copy = pltpu.make_async_copy(
                    array.at[layer, source, :], ref.at[:, pl.ds(lane, width)], sem
                )
                copy.start()
                copies.append(copy)
    for copy in late:
        copy.wait()
    at, lane = 0, 2 * layers * width
    for ref in packed:
        size = ref.shape[0]
        value = wide[at : at + size, :]
        high = value.astype(jnp.bfloat16)
        ref[:, lane : lane + out] = high
        ref[:, lane + out : lane + 2 * out] = (
            value - high.astype(jnp.float32)
        ).astype(jnp.bfloat16)
        at += size
    for copy in copies:
        copy.wait()


def pack(act, grad, targets, sizes, takes):
    layers, rows, width = act.shape
    out = targets.shape[1]
    lanes = 2 * layers * width + 2 * out
    return pl.pallas_call(
        functools.partial(pack_kernel, takes),
        out_shape=[jax.ShapeDtypeStruct((s, lanes), jnp.bfloat16) for s in sizes]
        + [TOKEN],
        in_specs=[pl.BlockSpec(memory_space=pltpu.HBM)] * 3,
        out_specs=[pl.BlockSpec(memory_space=pltpu.VMEM)] * (len(sizes) + 1),
        scratch_shapes=[
            pltpu.VMEM((sum(sizes), out), jnp.float32),
            pltpu.SemaphoreType.DMA(()),
            pltpu.SemaphoreType.DMA(()),
        ],
        compiler_params=pltpu.CompilerParams(vmem_limit_bytes=SCOPED_LIMIT),
    )(act, grad, targets)


def build(layers, scale, low, high, data, kernel):
    width = data.shape[1] // (2 * layers)
    for at in range(low, high, TILE):
        cols = slice(at, at + TILE)
        for row_at in range(0, at + TILE, TILE):
            rows = slice(row_at, row_at + TILE)
            total = None
            for layer in range(layers):
                a = slice(layer * width, (layer + 1) * width)
                g = slice((layers + layer) * width, (layers + layer + 1) * width)
                term = gram_pair(data[rows, a], data[cols, a]) * gram_pair(
                    data[rows, g], data[cols, g]
                )
                total = term if total is None else total + term
            block = (total * (1.0 / scale)).astype(jnp.bfloat16)
            kernel[rows, cols] = block
            if row_at != at:
                kernel[cols, rows] = block.T


def begin(low, high, kernel, residual, squashed):
    for at in range(low, high, TILE):
        cols = slice(at, at + TILE)
        squashed[cols, :] = jnp.tanh(residual[cols, :]).astype(jnp.bfloat16)
    for at in range(0, high, TILE):
        rows = slice(at, at + TILE)
        cols = slice(low if at < low else 0, high)
        residual[rows, :] -= RATE * jnp.dot(
            kernel[rows, cols], squashed[cols, :], preferred_element_type=jnp.float32
        )


def unpack_block(act, grad, low, data):
    layers, rows, width = act.shape
    for layer in range(layers):
        for side, array in enumerate((act, grad)):
            lane = (side * layers + layer) * width
            data[low : low + rows, lane : lane + width] = array[layer]


def unpack_pieces(pieces, low, data, residual):
    sketch, out = data.shape[1], residual.shape[1]
    for piece in pieces:
        high = low + piece.shape[0]
        data[low:high, :] = piece[:, :sketch]
        residual[low:high, :] = piece[:, sketch : sketch + out].astype(
            jnp.float32
        ) + piece[:, sketch + out :].astype(jnp.float32)
        low = high
    return low


def first_kernel(layers, scale, *refs):
    block, beside, state = refs[:3], refs[3:6], refs[7:11]
    token, sem = refs[11:]
    data, kernel, residual, squashed = state
    act, grad, targets = block
    rows, width = act.shape[1:]
    copies = [pltpu.make_async_copy(targets, residual.at[pl.ds(0, rows), :], sem)]
    for layer in range(layers):
        for side, array in enumerate((act, grad)):
            lane = (side * layers + layer) * width
            copies.append(
                pltpu.make_async_copy(
                    array.at[layer], data.at[pl.ds(0, rows), pl.ds(lane, width)], sem
                )
            )
    for copy in copies:
        copy.start()
    unpack_block(*beside[:2], rows, data)
    residual[rows : 2 * rows, :] = beside[2][...]
    for copy in copies:
        copy.wait()
    build(layers, scale, 0, 2 * rows, data, kernel)
    begin(0, 2 * rows, kernel, residual, squashed)
    token[...] = jnp.zeros_like(token)


def stage_kernel(layers, scale, low, count, *refs):
    pieces, state, token = refs[:count], refs[-5:-1], refs[-1]
    data, kernel, residual, squashed = state
    high = unpack_pieces(pieces, low, data, residual)
    build(layers, scale, low, high, data, kernel)
    begin(low, high, kernel, residual, squashed)
    token[...] = jnp.zeros_like(token)


def last_kernel(layers, scale, low, count, *refs):
    pieces, state = refs[:count], refs[count : count + 4]
    result, other = refs[count + 4 :]
    data, kernel, residual, squashed = state
    share = result.shape[0]
    high = unpack_pieces(pieces, low, data, residual)
    build(layers, scale, low, high, data, kernel)
    for at in range(low, high, TILE):
        cols = slice(at, at + TILE)
        squashed[cols, :] = jnp.tanh(residual[cols, :]).astype(jnp.bfloat16)
    for at in range(0, high, TILE):
        rows, cols = slice(at, at + TILE), slice(low if at < low else 0, high)
        value = residual[rows, :] - RATE * jnp.dot(
            kernel[rows, cols], squashed[cols, :], preferred_element_type=jnp.float32
        )
        residual[rows, :] = value
        other[rows, :] = jnp.tanh(value).astype(jnp.bfloat16)
    panels = (squashed, other)
    for step in range(1, ITERS - 1):
        now, later = panels[step % 2], panels[(step + 1) % 2]
        for at in range(0, high, TILE):
            rows = slice(at, at + TILE)
            update = jnp.dot(
                kernel[rows, :], now[...], preferred_element_type=jnp.float32
            )
            value = residual[rows, :] - RATE * update
            residual[rows, :] = value
            later[rows, :] = jnp.tanh(value).astype(jnp.bfloat16)
    place = lax.axis_index("col")
    mine = pl.ds(pl.multiple_of(place * share, share), share)
    update = jnp.dot(
        kernel[mine, :],
        panels[(ITERS - 1) % 2][...],
        preferred_element_type=jnp.float32,
    )
    result[...] = residual[mine, :] - RATE * update


def hold_kernel(*refs):
    pass


IN_VMEM = pl.BlockSpec(memory_space=pltpu.VMEM)
IN_HBM = pl.BlockSpec(memory_space=pltpu.HBM)
PARAMS = pltpu.CompilerParams(vmem_limit_bytes=SCOPED_LIMIT)
SMALL = pltpu.CompilerParams(vmem_limit_bytes=SCOPED_LIMIT // 4)
TOKEN = jax.ShapeDtypeStruct((8, 128), jnp.float32)


def cost(layers, width, out, low, high):
    grown = high * high - low * low
    return pl.CostEstimate(
        flops=grown * (2 * layers * width + 2 * out),
        bytes_accessed=grown,
        transcendentals=(high - low) * out,
    )


def state_shapes(examples, sketch, out):
    return [
        pltpu.VMEM((examples, sketch), jnp.bfloat16),
        pltpu.VMEM((examples, examples), jnp.bfloat16),
        pltpu.VMEM((examples, out), jnp.float32),
        pltpu.VMEM((examples, out), jnp.bfloat16),
    ]


def after(value, *tokens):
    return pl.pallas_call(
        hold_kernel,
        out_shape=jax.ShapeDtypeStruct(value.shape, value.dtype),
        in_specs=[IN_HBM] * (1 + len(tokens)),
        out_specs=IN_HBM,
        input_output_aliases={0: 0},
        compiler_params=SMALL,
    )(value, *tokens)


def join_kernel(count, *refs):
    joined, at = refs[-1], 0
    for piece in refs[:count]:
        joined[at : at + piece.shape[0], :] = piece[...]
        at += piece.shape[0]


def join(pieces, *tokens):
    shape = sum(piece.shape[0] for piece in pieces), pieces[0].shape[1]
    return pl.pallas_call(
        functools.partial(join_kernel, len(pieces)),
        out_shape=jax.ShapeDtypeStruct(shape, pieces[0].dtype),
        in_specs=[IN_VMEM] * len(pieces) + [IN_HBM] * len(tokens),
        out_specs=IN_VMEM,
        compiler_params=SMALL,
    )(*pieces, *tokens)


def whole_body(act_sketch, grad_sketch, targets):
    row_count = lax.axis_size("row")
    col_count = lax.axis_size("col")
    layers, rows, width = act_sketch.shape
    out = targets.shape[1]
    examples = rows * row_count
    share = rows // col_count
    scale = width * math.sqrt(examples) / 4.0
    quarter, eighth = rows // 4, rows // 8

    def twin(value):
        return lax.ppermute(value, "row", [(i, i ^ 1) for i in range(row_count)])

    def across(value):
        return lax.ppermute(value, "row", [(i, i ^ 2) for i in range(row_count)])

    def near(value):
        return lax.ppermute(value, "col", [(i, i ^ 1) for i in range(col_count)])

    def far(value):
        return lax.ppermute(value, "col", [(i, i ^ 2) for i in range(col_count)])

    shapes = state_shapes(examples, 2 * layers * width, out)

    def stage(state, low, pieces, *tokens):
        count = len(pieces)
        *state, token = pl.pallas_call(
            functools.partial(stage_kernel, layers, scale, low, count),
            out_shape=[*shapes, TOKEN],
            in_specs=[IN_VMEM] * (count + 4) + [IN_HBM] * len(tokens),
            out_specs=[IN_VMEM] * 5,
            input_output_aliases={count + i: i for i in range(4)},
            compiler_params=PARAMS,
        )(*pieces, *state, *tokens)
        return state, token

    own = [
        pltpu.with_memory_space_constraint(array, pltpu.HBM)
        for array in (act_sketch, grad_sketch, targets)
    ]
    first, second, third, token = pack(
        *own,
        (eighth, eighth, quarter),
        ((0, 0), (0, eighth), (1, 0)),
    )
    first, second = across(first), across(second)
    beside = twin(act_sketch), twin(grad_sketch), twin(targets)
    third = across(third)
    *state, token = pl.pallas_call(
        functools.partial(first_kernel, layers, scale),
        out_shape=[*shapes, TOKEN],
        in_specs=[IN_HBM] * 3 + [IN_VMEM] * 3 + [IN_HBM],
        out_specs=[IN_VMEM] * 5,
        scratch_shapes=[pltpu.SemaphoreType.DMA(())],
        compiler_params=PARAMS,
        cost_estimate=cost(layers, width, out, 0, 2 * rows),
    )(*own, *beside, token)

    first, second = after(first, token), after(second, token)
    near_first, far_first = near(first), far(first)
    near_second, far_second = near(second), far(second)
    low = 2 * rows
    four = [first, second, near_first, far_first]
    state, token = stage(state, low, four + [twin(piece) for piece in four])
    low += 4 * quarter
    last = join([near_second, far_second], token)
    third = after(third, token)
    state, token = stage(state, low, [third, twin(third)])
    low += 2 * quarter
    pieces = last
    pieces = [pieces, twin(pieces)]
    count = len(pieces)
    return pl.pallas_call(
        functools.partial(last_kernel, layers, scale, low, count),
        out_shape=jax.ShapeDtypeStruct((share, out), jnp.float32),
        in_specs=[IN_VMEM] * (count + 4),
        out_specs=IN_VMEM,
        scratch_shapes=[pltpu.VMEM((examples, out), jnp.bfloat16)],
        compiler_params=PARAMS,
    )(*pieces, *state)


def fits(mesh, act_sketch, targets):
    layers, examples, width = act_sketch.shape
    row_count, col_count = mesh.shape["row"], mesh.shape["col"]
    state = examples * (2 * examples + 4 * layers * width + 6 * targets.shape[1])
    return (
        state <= STATE_LIMIT
        and row_count == 4
        and col_count % 4 == 0
        and examples % (row_count * 2 * TILE) == 0
        and examples % (row_count * col_count * 16) == 0
    )


def solution(mesh):
    def step(act_sketch, grad_sketch, targets):
        body = whole_body if fits(mesh, act_sketch, targets) else split_body
        return jax.shard_map(
            body,
            mesh=mesh,
            in_specs=(P(None, "row", None), P(None, "row", None), P("row", None)),
            out_specs=P(("row", "col"), None),
            check_vma=False,
        )(act_sketch, grad_sketch, targets)

    return step
```

```python
import functools
import math

import jax
import jax.numpy as jnp
from jax import lax
from jax.experimental import pallas as pl
from jax.experimental.pallas import tpu as pltpu
from jax.sharding import PartitionSpec as P

ITERS = 8
RATE = 0.05
TILE = 256
STATE_LIMIT = 32 * 2**20
SCOPED_LIMIT = 16 * 2**20
NT = (((1,), (1,)), ((), ()))


def broadcast(value, axis, source):
    kept = jnp.where(lax.axis_index(axis) == source, value, 0).astype(value.dtype)
    return lax.psum(kept, axis)


def gram_pair(left, right):
    return lax.dot_general(left, right, NT, preferred_element_type=jnp.float32)


def split_body(act_sketch, grad_sketch, targets):
    row_count = lax.axis_size("row")
    col_count = lax.axis_size("col")
    ratio = col_count // row_count
    examples = targets.shape[0]
    col_block = examples // ratio
    share_rows = examples // col_count
    col_place = lax.axis_index("col")
    root = col_place // ratio
    offset = col_place % ratio * col_block
    scale = act_sketch.shape[2] * math.sqrt(examples * row_count) / 4.0

    def pick(array, dim):
        return lax.dynamic_slice_in_dim(array, offset, col_block, dim)

    act_cols, grad_cols = (
        broadcast(pick(act_sketch, 1), "row", root),
        broadcast(pick(grad_sketch, 1), "row", root),
    )
    total = jnp.zeros((examples, col_block), jnp.float32)
    for layer in range(act_sketch.shape[0]):
        act_gram = gram_pair(act_sketch[layer], act_cols[layer])
        grad_gram = gram_pair(grad_sketch[layer], grad_cols[layer])
        total = total + act_gram * grad_gram
    kernel = (total / scale).astype(jnp.bfloat16)
    state = targets
    for step in range(ITERS):
        panel = broadcast(
            jnp.tanh(pick(state, 0)).astype(jnp.bfloat16), "row", root
        )
        partial_value = jnp.dot(kernel, panel, preferred_element_type=jnp.float32)
        summed = lax.psum(partial_value, "col")
        state = state - RATE * summed
    return lax.dynamic_slice_in_dim(state, col_place * share_rows, share_rows, 0)


def kind_of(place):
    upper = (place // 2) % 2
    return (place % 2 + upper) % 2 * 2 + upper


def pack_kernel(takes, act, grad, targets, *refs):
    count = len(takes)
    packed, (token, wide, sem, wide_sem) = refs[:count], refs[count:]
    token[...] = jnp.zeros_like(token)
    layers, rows, width = act.shape
    out = targets.shape[1]
    quarter = rows // 4
    kind = kind_of(lax.axis_index("col"))
    copies, late, at = [], [], 0
    for ref, (flip, skip) in zip(packed, takes):
        size = ref.shape[0]
        quarter_at = (kind + flip - 2 * flip * (kind % 2)) * quarter + skip
        source = pl.ds(pl.multiple_of(quarter_at, 16), size)
        copy = pltpu.make_async_copy(
            targets.at[source, :], wide.at[pl.ds(at, size), :], wide_sem
        )
        copy.start()
        late.append(copy)
        at += size
        for layer in range(layers):
            for side, array in enumerate((act, grad)):
                lane = (side * layers + layer) * width
                copy = pltpu.make_async_copy(
                    array.at[layer, source, :], ref.at[:, pl.ds(lane, width)], sem
                )
                copy.start()
                copies.append(copy)
    for copy in late:
        copy.wait()
    at, lane = 0, 2 * layers * width
    for ref in packed:
        size = ref.shape[0]
        value = wide[at : at + size, :]
        high = value.astype(jnp.bfloat16)
        ref[:, lane : lane + out] = high
        ref[:, lane + out : lane + 2 * out] = (
            value - high.astype(jnp.float32)
        ).astype(jnp.bfloat16)
        at += size
    for copy in copies:
        copy.wait()


def pack(act, grad, targets, sizes, takes):
    layers, rows, width = act.shape
    out = targets.shape[1]
    lanes = 2 * layers * width + 2 * out
    return pl.pallas_call(
        functools.partial(pack_kernel, takes),
        out_shape=[jax.ShapeDtypeStruct((s, lanes), jnp.bfloat16) for s in sizes]
        + [TOKEN],
        in_specs=[pl.BlockSpec(memory_space=pltpu.HBM)] * 3,
        out_specs=[pl.BlockSpec(memory_space=pltpu.VMEM)] * (len(sizes) + 1),
        scratch_shapes=[
            pltpu.VMEM((sum(sizes), out), jnp.float32),
            pltpu.SemaphoreType.DMA(()),
            pltpu.SemaphoreType.DMA(()),
        ],
        compiler_params=pltpu.CompilerParams(vmem_limit_bytes=SCOPED_LIMIT),
    )(act, grad, targets)


def tiles(low, high):
    return [(at, min(at + TILE, high)) for at in range(low, high, TILE)]


def build(layers, scale, low, high, data, kernel):
    width = data.shape[1] // (2 * layers)
    for tile in tiles(low, high):
        cols = slice(*tile)
        for other in [*tiles(0, tile[0]), tile]:
            rows = slice(*other)
            total = None
            for layer in range(layers):
                a = slice(layer * width, (layer + 1) * width)
                g = slice((layers + layer) * width, (layers + layer + 1) * width)
                term = gram_pair(data[rows, a], data[cols, a]) * gram_pair(
                    data[rows, g], data[cols, g]
                )
                total = term if total is None else total + term
            block = (total * (1.0 / scale)).astype(jnp.bfloat16)
            kernel[rows, cols] = block
            if other != tile:
                kernel[cols, rows] = block.T


def begin(low, high, kernel, residual, squashed):
    for tile in tiles(low, high):
        cols = slice(*tile)
        squashed[cols, :] = jnp.tanh(residual[cols, :]).astype(jnp.bfloat16)
    for tile in tiles(0, low) + tiles(low, high):
        rows, cols = slice(*tile), slice(low if tile[0] < low else 0, high)
        residual[rows, :] -= RATE * jnp.dot(
            kernel[rows, cols], squashed[cols, :], preferred_element_type=jnp.float32
        )


def unpack_block(act, grad, low, data):
    layers, rows, width = act.shape
    for layer in range(layers):
        for side, array in enumerate((act, grad)):
            lane = (side * layers + layer) * width
            data[low : low + rows, lane : lane + width] = array[layer]


def unpack_pieces(pieces, low, data, residual):
    sketch, out = data.shape[1], residual.shape[1]
    for piece in pieces:
        high = low + piece.shape[0]
        data[low:high, :] = piece[:, :sketch]
        residual[low:high, :] = piece[:, sketch : sketch + out].astype(
            jnp.float32
        ) + piece[:, sketch + out :].astype(jnp.float32)
        low = high
    return low


def first_kernel(layers, scale, *refs):
    block, beside, state = refs[:3], refs[3:6], refs[7:11]
    token, sem = refs[11:]
    data, kernel, residual, squashed = state
    act, grad, targets = block
    rows, width = act.shape[1:]
    copies = [pltpu.make_async_copy(targets, residual.at[pl.ds(0, rows), :], sem)]
    for layer in range(layers):
        for side, array in enumerate((act, grad)):
            lane = (side * layers + layer) * width
            copies.append(
                pltpu.make_async_copy(
                    array.at[layer], data.at[pl.ds(0, rows), pl.ds(lane, width)], sem
                )
            )
    for copy in copies:
        copy.start()
    unpack_block(*beside[:2], rows, data)
    residual[rows : 2 * rows, :] = beside[2][...]
    for copy in copies:
        copy.wait()
    build(layers, scale, 0, 2 * rows, data, kernel)
    begin(0, 2 * rows, kernel, residual, squashed)
    token[...] = jnp.zeros_like(token)


def stage_kernel(layers, scale, low, count, sums, *refs):
    pieces, state, token = refs[:count], refs[-5:-1], refs[-1]
    data, kernel, residual, squashed = state
    high = unpack_pieces(pieces, low, data, residual)
    build(layers, scale, low, high, data, kernel)
    if sums:
        begin(low, high, kernel, residual, squashed)
    token[...] = jnp.zeros_like(token)


def last_kernel(layers, scale, start, low, count, *refs):
    pieces, state = refs[:count], refs[count : count + 4]
    result, other = refs[count + 4 :]
    data, kernel, residual, squashed = state
    share = result.shape[0]
    high = unpack_pieces(pieces, low, data, residual)
    build(layers, scale, low, high, data, kernel)
    for tile in tiles(start, high):
        cols = slice(*tile)
        squashed[cols, :] = jnp.tanh(residual[cols, :]).astype(jnp.bfloat16)
    for tile in tiles(0, start) + tiles(start, high):
        rows, cols = slice(*tile), slice(start if tile[0] < start else 0, high)
        value = residual[rows, :] - RATE * jnp.dot(
            kernel[rows, cols], squashed[cols, :], preferred_element_type=jnp.float32
        )
        residual[rows, :] = value
        other[rows, :] = jnp.tanh(value).astype(jnp.bfloat16)
    panels = (squashed, other)
    for step in range(1, ITERS - 1):
        now, later = panels[step % 2], panels[(step + 1) % 2]
        for at in range(0, high, 4 * TILE):
            rows = slice(at, at + 4 * TILE)
            update = jnp.dot(
                kernel[rows, :], now[...], preferred_element_type=jnp.float32
            )
            value = residual[rows, :] - RATE * update
            residual[rows, :] = value
            later[rows, :] = jnp.tanh(value).astype(jnp.bfloat16)
    place = lax.axis_index("col")
    mine = pl.ds(pl.multiple_of(place * share, share), share)
    update = jnp.dot(
        kernel[mine, :],
        panels[(ITERS - 1) % 2][...],
        preferred_element_type=jnp.float32,
    )
    result[...] = residual[mine, :] - RATE * update


def hold_kernel(*refs):
    pass


IN_VMEM = pl.BlockSpec(memory_space=pltpu.VMEM)
IN_HBM = pl.BlockSpec(memory_space=pltpu.HBM)
PARAMS = pltpu.CompilerParams(vmem_limit_bytes=SCOPED_LIMIT)
SMALL = pltpu.CompilerParams(vmem_limit_bytes=SCOPED_LIMIT // 4)
TOKEN = jax.ShapeDtypeStruct((8, 128), jnp.float32)


def cost(layers, width, out, low, high):
    grown = high * high - low * low
    return pl.CostEstimate(
        flops=grown * (2 * layers * width + 2 * out),
        bytes_accessed=grown,
        transcendentals=(high - low) * out,
    )


def state_shapes(examples, sketch, out):
    return [
        pltpu.VMEM((examples, sketch), jnp.bfloat16),
        pltpu.VMEM((examples, examples), jnp.bfloat16),
        pltpu.VMEM((examples, out), jnp.float32),
        pltpu.VMEM((examples, out), jnp.bfloat16),
    ]


def after(value, *tokens):
    return pl.pallas_call(
        hold_kernel,
        out_shape=jax.ShapeDtypeStruct(value.shape, value.dtype),
        in_specs=[IN_HBM] * (1 + len(tokens)),
        out_specs=IN_HBM,
        input_output_aliases={0: 0},
        compiler_params=SMALL,
    )(value, *tokens)


def join_kernel(count, *refs):
    joined, at = refs[-1], 0
    for piece in refs[:count]:
        joined[at : at + piece.shape[0], :] = piece[...]
        at += piece.shape[0]


def join(pieces, *tokens):
    shape = sum(piece.shape[0] for piece in pieces), pieces[0].shape[1]
    return pl.pallas_call(
        functools.partial(join_kernel, len(pieces)),
        out_shape=jax.ShapeDtypeStruct(shape, pieces[0].dtype),
        in_specs=[IN_VMEM] * len(pieces) + [IN_HBM] * len(tokens),
        out_specs=IN_VMEM,
        compiler_params=SMALL,
    )(*pieces, *tokens)


def whole_body(act_sketch, grad_sketch, targets):
    row_count = lax.axis_size("row")
    col_count = lax.axis_size("col")
    layers, rows, width = act_sketch.shape
    out = targets.shape[1]
    examples = rows * row_count
    share = rows // col_count
    scale = width * math.sqrt(examples) / 4.0
    quarter, eighth = rows // 4, rows // 8

    def twin(value):
        return lax.ppermute(value, "row", [(i, i ^ 1) for i in range(row_count)])

    def across(value):
        return lax.ppermute(value, "row", [(i, i ^ 2) for i in range(row_count)])

    def near(value):
        return lax.ppermute(value, "col", [(i, i ^ 1) for i in range(col_count)])

    def far(value):
        return lax.ppermute(value, "col", [(i, i ^ 2) for i in range(col_count)])

    shapes = state_shapes(examples, 2 * layers * width, out)

    def stage(state, low, pieces, sums=True):
        count = len(pieces)
        *state, token = pl.pallas_call(
            functools.partial(stage_kernel, layers, scale, low, count, sums),
            out_shape=[*shapes, TOKEN],
            in_specs=[IN_VMEM] * (count + 4),
            out_specs=[IN_VMEM] * 5,
            input_output_aliases={count + i: i for i in range(4)},
            compiler_params=PARAMS,
        )(*pieces, *state)
        return state, token

    own = [
        pltpu.with_memory_space_constraint(array, pltpu.HBM)
        for array in (act_sketch, grad_sketch, targets)
    ]
    first, second, third, token = pack(
        *own,
        (eighth, eighth, quarter),
        ((0, 0), (0, eighth), (1, 0)),
    )
    first, second = across(first), across(second)
    beside = twin(act_sketch), twin(grad_sketch), twin(targets)
    third = across(third)
    *state, token = pl.pallas_call(
        functools.partial(first_kernel, layers, scale),
        out_shape=[*shapes, TOKEN],
        in_specs=[IN_HBM] * 3 + [IN_VMEM] * 3 + [IN_HBM],
        out_specs=[IN_VMEM] * 5,
        scratch_shapes=[pltpu.SemaphoreType.DMA(())],
        compiler_params=PARAMS,
        cost_estimate=cost(layers, width, out, 0, 2 * rows),
    )(*own, *beside, token)

    first, second = after(first, token), after(second, token)
    near_first, far_first = near(first), far(first)
    near_second, far_second = near(second), far(second)
    low = 2 * rows
    four = [first, second, near_first, far_first]
    state, token = stage(state, low, four + [twin(piece) for piece in four])
    low += 2 * sum(piece.shape[0] for piece in four)
    last = join([near_second, far_second], token)
    third = after(third, token)
    state, token = stage(state, low, [third, twin(third)], sums=False)
    start, low = low, low + 2 * quarter
    pieces = last
    pieces = [pieces, twin(pieces)]
    count = len(pieces)
    return pl.pallas_call(
        functools.partial(last_kernel, layers, scale, start, low, count),
        out_shape=jax.ShapeDtypeStruct((share, out), jnp.float32),
        in_specs=[IN_VMEM] * (count + 4),
        out_specs=IN_VMEM,
        scratch_shapes=[pltpu.VMEM((examples, out), jnp.bfloat16)],
        compiler_params=PARAMS,
    )(*pieces, *state)


def fits(mesh, act_sketch, targets):
    layers, examples, width = act_sketch.shape
    row_count, col_count = mesh.shape["row"], mesh.shape["col"]
    state = examples * (2 * examples + 4 * layers * width + 6 * targets.shape[1])
    return (
        state <= STATE_LIMIT
        and row_count == 4
        and col_count % 4 == 0
        and examples % (row_count * 2 * TILE) == 0
        and examples % (row_count * col_count * 16) == 0
    )


def solution(mesh):
    def step(act_sketch, grad_sketch, targets):
        body = whole_body if fits(mesh, act_sketch, targets) else split_body
        return jax.shard_map(
            body,
            mesh=mesh,
            in_specs=(P(None, "row", None), P(None, "row", None), P("row", None)),
            out_specs=P(("row", "col"), None),
            check_vma=False,
        )(act_sketch, grad_sketch, targets)

    return step
```

```python
import functools
import math

import jax
import jax.numpy as jnp
from jax import lax
from jax.experimental import pallas as pl
from jax.experimental.pallas import tpu as pltpu
from jax.sharding import PartitionSpec as P

ITERS = 8
RATE = 0.05
TILE = 256
STATE_LIMIT = 32 * 2**20
SCOPED_LIMIT = 16 * 2**20
NT = (((1,), (1,)), ((), ()))


def broadcast(value, axis, source):
    kept = jnp.where(lax.axis_index(axis) == source, value, 0).astype(value.dtype)
    return lax.psum(kept, axis)


def gram_pair(left, right):
    return lax.dot_general(left, right, NT, preferred_element_type=jnp.float32)


def split_body(act_sketch, grad_sketch, targets):
    row_count = lax.axis_size("row")
    col_count = lax.axis_size("col")
    ratio = col_count // row_count
    examples = targets.shape[0]
    col_block = examples // ratio
    share_rows = examples // col_count
    col_place = lax.axis_index("col")
    root = col_place // ratio
    offset = col_place % ratio * col_block
    scale = act_sketch.shape[2] * math.sqrt(examples * row_count) / 4.0

    def pick(array, dim):
        return lax.dynamic_slice_in_dim(array, offset, col_block, dim)

    act_cols, grad_cols = (
        broadcast(pick(act_sketch, 1), "row", root),
        broadcast(pick(grad_sketch, 1), "row", root),
    )
    total = jnp.zeros((examples, col_block), jnp.float32)
    for layer in range(act_sketch.shape[0]):
        act_gram = gram_pair(act_sketch[layer], act_cols[layer])
        grad_gram = gram_pair(grad_sketch[layer], grad_cols[layer])
        total = total + act_gram * grad_gram
    kernel = (total / scale).astype(jnp.bfloat16)
    state = targets
    for step in range(ITERS):
        panel = broadcast(
            jnp.tanh(pick(state, 0)).astype(jnp.bfloat16), "row", root
        )
        partial_value = jnp.dot(kernel, panel, preferred_element_type=jnp.float32)
        summed = lax.psum(partial_value, "col")
        state = state - RATE * summed
    return lax.dynamic_slice_in_dim(state, col_place * share_rows, share_rows, 0)


def kind_of(place):
    upper = (place // 2) % 2
    return (place % 2 + upper) % 2 * 2 + upper


def pack_kernel(takes, act, grad, targets, *refs):
    count = len(takes)
    packed, (token, wide, sem, wide_sem) = refs[:count], refs[count:]
    token[...] = jnp.zeros_like(token)
    layers, rows, width = act.shape
    out = targets.shape[1]
    quarter = rows // 4
    kind = kind_of(lax.axis_index("col"))
    copies, late, at = [], [], 0
    for ref, (flip, skip) in zip(packed, takes):
        size = ref.shape[0]
        quarter_at = (kind + flip - 2 * flip * (kind % 2)) * quarter + skip
        source = pl.ds(pl.multiple_of(quarter_at, 16), size)
        copy = pltpu.make_async_copy(
            targets.at[source, :], wide.at[pl.ds(at, size), :], wide_sem
        )
        copy.start()
        late.append(copy)
        at += size
        for layer in range(layers):
            for side, array in enumerate((act, grad)):
                lane = (side * layers + layer) * width
                copy = pltpu.make_async_copy(
                    array.at[layer, source, :], ref.at[:, pl.ds(lane, width)], sem
                )
                copy.start()
                copies.append(copy)
    for copy in late:
        copy.wait()
    at, lane = 0, 2 * layers * width
    for ref in packed:
        size = ref.shape[0]
        value = wide[at : at + size, :]
        high = value.astype(jnp.bfloat16)
        ref[:, lane : lane + out] = high
        ref[:, lane + out : lane + 2 * out] = (
            value - high.astype(jnp.float32)
        ).astype(jnp.bfloat16)
        at += size
    for copy in copies:
        copy.wait()


def pack(act, grad, targets, sizes, takes):
    layers, rows, width = act.shape
    out = targets.shape[1]
    lanes = 2 * layers * width + 2 * out
    return pl.pallas_call(
        functools.partial(pack_kernel, takes),
        out_shape=[jax.ShapeDtypeStruct((s, lanes), jnp.bfloat16) for s in sizes]
        + [TOKEN],
        in_specs=[pl.BlockSpec(memory_space=pltpu.HBM)] * 3,
        out_specs=[pl.BlockSpec(memory_space=pltpu.VMEM)] * (len(sizes) + 1),
        scratch_shapes=[
            pltpu.VMEM((sum(sizes), out), jnp.float32),
            pltpu.SemaphoreType.DMA(()),
            pltpu.SemaphoreType.DMA(()),
        ],
        compiler_params=pltpu.CompilerParams(vmem_limit_bytes=SCOPED_LIMIT),
    )(act, grad, targets)


def tiles(low, high, size=TILE):
    return [(at, min(at + size, high)) for at in range(low, high, size)]


def build(layers, scale, low, high, data, kernel):
    width = data.shape[1] // (2 * layers)
    for tile in tiles(low, high):
        cols = slice(*tile)
        for other in [*tiles(0, tile[0]), tile]:
            rows = slice(*other)
            total = None
            for layer in range(layers):
                a = slice(layer * width, (layer + 1) * width)
                g = slice((layers + layer) * width, (layers + layer + 1) * width)
                term = gram_pair(data[rows, a], data[cols, a]) * gram_pair(
                    data[rows, g], data[cols, g]
                )
                total = term if total is None else total + term
            block = (total * (1.0 / scale)).astype(jnp.bfloat16)
            kernel[rows, cols] = block
            if other != tile:
                kernel[cols, rows] = block.T


def begin(low, high, kernel, residual, squashed):
    for tile in tiles(low, high):
        cols = slice(*tile)
        squashed[cols, :] = jnp.tanh(residual[cols, :]).astype(jnp.bfloat16)
    for tile in tiles(0, low) + tiles(low, high):
        rows, cols = slice(*tile), slice(low if tile[0] < low else 0, high)
        residual[rows, :] -= RATE * jnp.dot(
            kernel[rows, cols], squashed[cols, :], preferred_element_type=jnp.float32
        )


def unpack_block(act, grad, low, data):
    layers, rows, width = act.shape
    for layer in range(layers):
        for side, array in enumerate((act, grad)):
            lane = (side * layers + layer) * width
            data[low : low + rows, lane : lane + width] = array[layer]


def unpack_pieces(pieces, low, data, residual):
    sketch, out = data.shape[1], residual.shape[1]
    for piece in pieces:
        high = low + piece.shape[0]
        data[low:high, :] = piece[:, :sketch]
        residual[low:high, :] = piece[:, sketch : sketch + out].astype(
            jnp.float32
        ) + piece[:, sketch + out :].astype(jnp.float32)
        low = high
    return low


def first_kernel(layers, scale, *refs):
    block, beside, state = refs[:3], refs[3:6], refs[7:11]
    token, sem = refs[11:]
    data, kernel, residual, squashed = state
    act, grad, targets = block
    rows, width = act.shape[1:]
    copies = [pltpu.make_async_copy(targets, residual.at[pl.ds(0, rows), :], sem)]
    for layer in range(layers):
        for side, array in enumerate((act, grad)):
            lane = (side * layers + layer) * width
            copies.append(
                pltpu.make_async_copy(
                    array.at[layer], data.at[pl.ds(0, rows), pl.ds(lane, width)], sem
                )
            )
    for copy in copies:
        copy.start()
    unpack_block(*beside[:2], rows, data)
    residual[rows : 2 * rows, :] = beside[2][...]
    for copy in copies:
        copy.wait()
    build(layers, scale, 0, 2 * rows, data, kernel)
    begin(0, 2 * rows, kernel, residual, squashed)
    token[...] = jnp.zeros_like(token)


def stage_kernel(layers, scale, low, count, sums, *refs):
    pieces, state, token = refs[:count], refs[-5:-1], refs[-1]
    data, kernel, residual, squashed = state
    high = unpack_pieces(pieces, low, data, residual)
    build(layers, scale, low, high, data, kernel)
    if sums:
        begin(low, high, kernel, residual, squashed)
    token[...] = jnp.zeros_like(token)


def last_kernel(layers, scale, start, low, count, *refs):
    pieces, state = refs[:count], refs[count : count + 4]
    result, other = refs[count + 4 :]
    data, kernel, residual, squashed = state
    share = result.shape[0]
    high = unpack_pieces(pieces, low, data, residual)
    build(layers, scale, low, high, data, kernel)
    for tile in tiles(start, high):
        cols = slice(*tile)
        squashed[cols, :] = jnp.tanh(residual[cols, :]).astype(jnp.bfloat16)
    for tile in tiles(0, start, 4 * TILE) + tiles(start, high, 4 * TILE):
        rows, cols = slice(*tile), slice(start if tile[0] < start else 0, high)
        value = residual[rows, :] - RATE * jnp.dot(
            kernel[rows, cols], squashed[cols, :], preferred_element_type=jnp.float32
        )
        residual[rows, :] = value
        other[rows, :] = jnp.tanh(value).astype(jnp.bfloat16)
    panels = (squashed, other)
    for step in range(1, ITERS - 1):
        now, later = panels[step % 2], panels[(step + 1) % 2]
        for at in range(0, high, 4 * TILE):
            rows = slice(at, at + 4 * TILE)
            update = jnp.dot(
                kernel[rows, :], now[...], preferred_element_type=jnp.float32
            )
            value = residual[rows, :] - RATE * update
            residual[rows, :] = value
            later[rows, :] = jnp.tanh(value).astype(jnp.bfloat16)
    place = lax.axis_index("col")
    mine = pl.ds(pl.multiple_of(place * share, share), share)
    update = jnp.dot(
        kernel[mine, :],
        panels[(ITERS - 1) % 2][...],
        preferred_element_type=jnp.float32,
    )
    result[...] = residual[mine, :] - RATE * update


def hold_kernel(*refs):
    pass


IN_VMEM = pl.BlockSpec(memory_space=pltpu.VMEM)
IN_HBM = pl.BlockSpec(memory_space=pltpu.HBM)
PARAMS = pltpu.CompilerParams(vmem_limit_bytes=SCOPED_LIMIT)
SMALL = pltpu.CompilerParams(vmem_limit_bytes=SCOPED_LIMIT // 4)
TOKEN = jax.ShapeDtypeStruct((8, 128), jnp.float32)


def cost(layers, width, out, low, high):
    grown = high * high - low * low
    return pl.CostEstimate(
        flops=grown * (2 * layers * width + 2 * out),
        bytes_accessed=grown,
        transcendentals=(high - low) * out,
    )


def state_shapes(examples, sketch, out):
    return [
        pltpu.VMEM((examples, sketch), jnp.bfloat16),
        pltpu.VMEM((examples, examples), jnp.bfloat16),
        pltpu.VMEM((examples, out), jnp.float32),
        pltpu.VMEM((examples, out), jnp.bfloat16),
    ]


def after(value, *tokens):
    return pl.pallas_call(
        hold_kernel,
        out_shape=jax.ShapeDtypeStruct(value.shape, value.dtype),
        in_specs=[IN_HBM] * (1 + len(tokens)),
        out_specs=IN_HBM,
        input_output_aliases={0: 0},
        compiler_params=SMALL,
    )(value, *tokens)


def join_kernel(count, *refs):
    joined, at = refs[-1], 0
    for piece in refs[:count]:
        joined[at : at + piece.shape[0], :] = piece[...]
        at += piece.shape[0]


def join(pieces, *tokens):
    shape = sum(piece.shape[0] for piece in pieces), pieces[0].shape[1]
    return pl.pallas_call(
        functools.partial(join_kernel, len(pieces)),
        out_shape=jax.ShapeDtypeStruct(shape, pieces[0].dtype),
        in_specs=[IN_VMEM] * len(pieces) + [IN_HBM] * len(tokens),
        out_specs=IN_VMEM,
        compiler_params=SMALL,
    )(*pieces, *tokens)


def whole_body(act_sketch, grad_sketch, targets):
    row_count = lax.axis_size("row")
    col_count = lax.axis_size("col")
    layers, rows, width = act_sketch.shape
    out = targets.shape[1]
    examples = rows * row_count
    share = rows // col_count
    scale = width * math.sqrt(examples) / 4.0
    quarter, eighth = rows // 4, rows // 8

    def twin(value):
        return lax.ppermute(value, "row", [(i, i ^ 1) for i in range(row_count)])

    def across(value):
        return lax.ppermute(value, "row", [(i, i ^ 2) for i in range(row_count)])

    def near(value):
        return lax.ppermute(value, "col", [(i, i ^ 1) for i in range(col_count)])

    def far(value):
        return lax.ppermute(value, "col", [(i, i ^ 2) for i in range(col_count)])

    shapes = state_shapes(examples, 2 * layers * width, out)

    def stage(state, low, pieces, sums=True):
        count = len(pieces)
        *state, token = pl.pallas_call(
            functools.partial(stage_kernel, layers, scale, low, count, sums),
            out_shape=[*shapes, TOKEN],
            in_specs=[IN_VMEM] * (count + 4),
            out_specs=[IN_VMEM] * 5,
            input_output_aliases={count + i: i for i in range(4)},
            compiler_params=PARAMS,
        )(*pieces, *state)
        return state, token

    own = [
        pltpu.with_memory_space_constraint(array, pltpu.HBM)
        for array in (act_sketch, grad_sketch, targets)
    ]
    first, second, third, token = pack(
        *own,
        (eighth, eighth, quarter),
        ((0, 0), (0, eighth), (1, 0)),
    )
    first, second = across(first), across(second)
    beside = twin(act_sketch), twin(grad_sketch), twin(targets)
    third = across(third)
    *state, token = pl.pallas_call(
        functools.partial(first_kernel, layers, scale),
        out_shape=[*shapes, TOKEN],
        in_specs=[IN_HBM] * 3 + [IN_VMEM] * 3 + [IN_HBM],
        out_specs=[IN_VMEM] * 5,
        scratch_shapes=[pltpu.SemaphoreType.DMA(())],
        compiler_params=PARAMS,
        cost_estimate=cost(layers, width, out, 0, 2 * rows),
    )(*own, *beside, token)

    first, second = after(first, token), after(second, token)
    near_first, far_first = near(first), far(first)
    near_second, far_second = near(second), far(second)
    low = 2 * rows
    four = [first, second, near_first, far_first]
    state, token = stage(state, low, four + [twin(piece) for piece in four])
    low += 2 * sum(piece.shape[0] for piece in four)
    last = join([near_second, far_second], token)
    third = after(third, token)
    state, token = stage(state, low, [third, twin(third)], sums=False)
    start, low = low, low + 2 * quarter
    pieces = last
    pieces = [pieces, twin(pieces)]
    count = len(pieces)
    return pl.pallas_call(
        functools.partial(last_kernel, layers, scale, start, low, count),
        out_shape=jax.ShapeDtypeStruct((share, out), jnp.float32),
        in_specs=[IN_VMEM] * (count + 4),
        out_specs=IN_VMEM,
        scratch_shapes=[pltpu.VMEM((examples, out), jnp.bfloat16)],
        compiler_params=PARAMS,
    )(*pieces, *state)


def fits(mesh, act_sketch, targets):
    layers, examples, width = act_sketch.shape
    row_count, col_count = mesh.shape["row"], mesh.shape["col"]
    state = examples * (2 * examples + 4 * layers * width + 6 * targets.shape[1])
    return (
        state <= STATE_LIMIT
        and row_count == 4
        and col_count % 4 == 0
        and examples % (row_count * 2 * TILE) == 0
        and examples % (row_count * col_count * 16) == 0
    )


def solution(mesh):
    def step(act_sketch, grad_sketch, targets):
        body = whole_body if fits(mesh, act_sketch, targets) else split_body
        return jax.shard_map(
            body,
            mesh=mesh,
            in_specs=(P(None, "row", None), P(None, "row", None), P("row", None)),
            out_specs=P(("row", "col"), None),
            check_vma=False,
        )(act_sketch, grad_sketch, targets)

    return step
```
